32 devices in a mesh: chan: 8 (over z, y), split: 4 (over x, core).
Axes of the slice: x: 2, y: 2, z: 4, core: 2. Of those that a mesh axis runs over, the one named last changes fastest.
Arguments:
- omega: bfloat16 [8, 2048, 2048], P('chan', 'split'), as said below
- hamil: bfloat16 [8, 2048, 2048], P('chan', 'split'), as said below
- pp_sign: float32 [8, 2048], P('chan', 'split'), may hold values from -1 to 1, as said below
- ph_sign: float32 [8, 2048], P('chan', 'split'), may hold values from -1 to 1, as said below
- row_coef: float32 [8, 2048], P('chan', 'split'), may hold values from -2 to 2
- col_coef: float32 [8, 2048], P('chan'), may hold values from -2 to 2
- col_perm: int32 [8, 2048], P('chan'), may hold values from 0 to 2047, each once within a row
- send_order: int32 [8, 2048], P('chan', 'split'), may hold values from 0 to 511, as said below
Outputs:
- z_out: bfloat16 [8, 2048, 2048], P('chan', 'split')
- one_body: float32 [2048], replicated
The draws below stay inside these ranges and needn't reach their ends.
Inputs may be any that keep to these rules, and one draw needn't show every extreme that they name: omega[c] is antisymmetric for every channel c. hamil[c] is symmetric for every channel c. `pp_sign`: every entry is -1, 0 or 1; nearly all are 1. `ph_sign`: every entry is -1, 0 or 1; each aligned block of 512 entries of a channel holds exactly 32 nonzero entries. `send_order`: for every channel, each aligned block of 512 entries is a permutation of 0 to 511.
All inputs are finite; a program needn't handle non-finite values.
Results may differ from the reference program's by a relative error of at most 0.0034.
Values may be sent and summed in bfloat16 or wider, within the bound.
A program may use at most 128 MiB of HBM per device.

```python
import math
import jax
import jax.numpy as jnp
from jax import lax

CHAN_WIDTH = 2048
CHANNELS = 8
ROWS_LOCAL = 512
ROW_SLOTS = 64
ACTIVE_ROWS = 32


def draw_omega(key, part):
    key = jax.random.fold_in(key, 11)
    shape = (CHANNELS, CHAN_WIDTH, CHAN_WIDTH)
    base = jax.random.normal(key, shape, jnp.float32)
    scale = (0.5 / CHAN_WIDTH) ** 0.5
    return ((base - jnp.swapaxes(base, 1, 2)) * scale).astype(jnp.bfloat16)


def draw_hamil(key, part):
    key = jax.random.fold_in(key, 23)
    shape = (CHANNELS, CHAN_WIDTH, CHAN_WIDTH)
    base = jax.random.normal(key, shape, jnp.float32)
    return ((base + jnp.swapaxes(base, 1, 2)) * 0.70710678).astype(jnp.bfloat16)


def draw_pp_sign(key, part):
    key = jax.random.fold_in(key, 31)
    values = jax.random.randint(key, (CHANNELS, CHAN_WIDTH), 0, 100)
    signs = jnp.where(values < 1, -1, jnp.where(values < 5, 0, 1))
    return signs.astype(jnp.float32)


def draw_ph_sign(key, part):
    key = jax.random.fold_in(key, 37)
    key_order, key_sign = jax.random.split(key)
    blocks = CHANNELS * (CHAN_WIDTH // ROWS_LOCAL)
    keys = jax.random.split(key_order, blocks)

    def one_block(block_key):
        return jax.random.permutation(block_key, ROWS_LOCAL)
    ranks = jax.vmap(one_block)(keys).reshape(CHANNELS, CHAN_WIDTH)
    flips = 2 * jax.random.randint(key_sign, (CHANNELS, CHAN_WIDTH), 0, 2) - 1
    signs = jnp.where(ranks < ACTIVE_ROWS, flips, 0)
    return signs.astype(jnp.float32)


def draw_send_order(key, part):
    key = jax.random.fold_in(key, 41)
    keys = jax.random.split(key, CHANNELS * (CHAN_WIDTH // ROWS_LOCAL))

    def one_block(block_key):
        return jax.random.permutation(block_key, ROWS_LOCAL)
    blocks = jax.vmap(one_block)(keys)
    return blocks.reshape(CHANNELS, CHAN_WIDTH).astype(jnp.int32)


def block_levels(stream_key, extent, cuts, smallest, high):
    level, own = 1.0, jax.random.fold_in(stream_key, 6)
    for axis_at, shards_of in cuts:
        draws = jnp.exp(jax.random.uniform(jax.random.fold_in(own, axis_at), (shards_of,), jnp.float32, smallest / len(cuts), high / len(cuts)))
        level = level * jnp.repeat(draws, extent[axis_at] // shards_of).reshape([-1 if axis == axis_at else 1 for axis in range(len(extent))])
    return level


def setup_inputs(seed: int = 0) -> dict:
    streams_of = jax.random.split(jax.random.key(seed), 9)
    return {
        "omega": draw_omega(jax.random.fold_in(streams_of[8], 71), 0),
        "hamil": draw_hamil(jax.random.fold_in(streams_of[8], 71), 0),
        "pp_sign": draw_pp_sign(jax.random.fold_in(streams_of[8], 71), 0),
        "ph_sign": draw_ph_sign(jax.random.fold_in(streams_of[8], 71), 0),
        "row_coef": jnp.clip(jax.random.uniform(streams_of[4], (CHANNELS, CHAN_WIDTH), jnp.float32, -2.0, 2.0) * block_levels(streams_of[4], (CHANNELS, CHAN_WIDTH), ((0, 8), (1, 4)), -0.4, 0.0), -2.0, 2.0),
        "col_coef": jnp.clip(jax.random.uniform(streams_of[5], (CHANNELS, CHAN_WIDTH), jnp.float32, -2.0, 2.0) * block_levels(streams_of[5], (CHANNELS, CHAN_WIDTH), ((0, 8),), -0.4, 0.0), -2.0, 2.0),
        "col_perm": jax.vmap(lambda own: jax.random.permutation(own, CHAN_WIDTH))(jax.random.split(streams_of[6], CHANNELS)).reshape((CHANNELS, CHAN_WIDTH)).astype(jnp.int32),
        "send_order": draw_send_order(jax.random.fold_in(streams_of[8], 71), 0),
    }


def reference(omega, hamil, pp_sign, ph_sign, row_coef, col_coef, col_perm, send_order):
    positions = jnp.arange(CHAN_WIDTH, dtype=jnp.int32)
    block_ids = positions // ROWS_LOCAL
    within = positions % ROWS_LOCAL
    group_ids = within // ROW_SLOTS
    slot_ids = within % ROW_SLOTS
    omega_flat = omega.reshape(CHANNELS * CHAN_WIDTH, CHAN_WIDTH)
    hamil_flat = hamil.reshape(CHANNELS * CHAN_WIDTH, CHAN_WIDTH)

    def ladder_one(packed):
        omega_block, hamil_block, signs = packed
        scaled = (signs[:, None] * hamil_block.astype(jnp.float32)).astype(jnp.bfloat16)
        half = jnp.dot(omega_block, scaled, preferred_element_type=jnp.float32)
        return half + half.T
    ladder = lax.map(ladder_one, (omega, hamil, pp_sign))

    def forward(chan_q):
        source_pos = block_ids * ROWS_LOCAL + chan_q * ROW_SLOTS + slot_ids
        source_row = block_ids * ROWS_LOCAL + send_order[group_ids, source_pos]
        flat_rows = (group_ids * CHAN_WIDTH + source_row).astype(jnp.int32)
        recv_o = jnp.take(omega_flat, flat_rows, axis=0)
        recv_h = jnp.take(hamil_flat, flat_rows, axis=0)
        perm_q = col_perm[chan_q]
        coefs = row_coef[chan_q][:, None] * col_coef[chan_q][None, :]
        bar_o = (coefs * recv_o[:, perm_q].astype(jnp.float32)).astype(jnp.bfloat16)
        bar_h = (coefs * recv_h[:, perm_q].astype(jnp.float32)).astype(jnp.bfloat16)
        row_signs = ph_sign[chan_q][:, None]
        right_o = (row_signs * bar_o.astype(jnp.float32)).astype(jnp.bfloat16)
        right_h = (row_signs * bar_h.astype(jnp.float32)).astype(jnp.bfloat16)
        ph_sum = jnp.dot(bar_o, right_h, preferred_element_type=jnp.float32)
        ph_sum = ph_sum - jnp.dot(bar_h, right_o, preferred_element_type=jnp.float32)
        inverse = jnp.zeros((CHAN_WIDTH,), jnp.int32).at[perm_q].set(positions)
        return (coefs * ph_sum)[:, inverse].astype(jnp.bfloat16)
    back_all = lax.map(forward, jnp.arange(CHANNELS, dtype=jnp.int32))
    back_flat = back_all.reshape(CHANNELS * CHAN_WIDTH, CHAN_WIDTH)

    def backward(packed):
        chan_c, ladder_block, signs = packed
        target = (block_ids * ROWS_LOCAL + send_order[chan_c]).astype(jnp.int32)
        source = (group_ids * CHAN_WIDTH + block_ids * ROWS_LOCAL + chan_c * ROW_SLOTS + slot_ids).astype(jnp.int32)
        rows_from = jnp.zeros((CHAN_WIDTH,), jnp.int32).at[target].set(source)
        total = ladder_block + jnp.take(back_flat, rows_from, axis=0).astype(jnp.float32)
        weight = (2 * (chan_c // 2) + 1).astype(jnp.float32)
        partial_sum = weight * jnp.dot(signs, total, precision=lax.Precision.HIGHEST)
        return (total.astype(jnp.bfloat16), partial_sum)
    z_out, partials = lax.map(backward, (jnp.arange(CHANNELS, dtype=jnp.int32), ladder, pp_sign))
    weight_sq = sum(((2 * (chan_pos // 2) + 1) ** 2 for chan_pos in range(CHANNELS)))
    one_body = lax.optimization_barrier(jnp.sum(partials, axis=0)) * (1.0 / math.sqrt(CHAN_WIDTH * weight_sq))
    return (z_out, one_body)
```

```python
import math

import jax
import jax.numpy as jnp
from jax import lax
from jax.sharding import PartitionSpec as P

F32, BF16 = jnp.float32, jnp.bfloat16


def dot(a, b):
    return jnp.dot(a, b, preferred_element_type=F32)


def prepare(omega, hamil, pp_sign, ph_sign, row_coef, col_coef, col_perm, send_order):
    chan_count = lax.axis_size("chan")
    _, height, breadth = omega.shape
    slots = height // chan_count
    active = height // 16
    me_c, me_s = lax.axis_index("chan"), lax.axis_index("split")
    sign = ph_sign[0]
    mask = sign != 0
    lower = jnp.arange(height)[:, None] <= jnp.arange(height)[None, :]
    rank = jnp.sum(jnp.where(lower & mask[:, None], 1, 0), axis=0) - 1
    rank = jnp.where(mask, rank, -1)
    pick = rank[None, :] == jnp.arange(active)[:, None]
    own_perm = lax.dynamic_slice(col_perm[0], (me_s * height,), (height,))
    own_cc = lax.dynamic_slice(col_coef[0], (me_s * height,), (height,))

    def picked(values):
        return jnp.sum(jnp.where(pick, values[None, :].astype(F32), 0.0), axis=1)

    pack = jnp.concatenate(
        [picked(own_perm), picked(own_cc), rank.astype(F32), pp_sign[0]]
    )
    packs = lax.all_gather(pack, ("chan", "split"), axis=0, tiled=False)
    packs = packs.reshape(chan_count, -1, pack.shape[0])
    cols = packs[:, :, :active].reshape(chan_count, -1).astype(jnp.int32)
    act_cc = lax.dynamic_index_in_dim(packs, me_c, 0, False)[:, active : 2 * active].reshape(-1)
    ranks = lax.dynamic_index_in_dim(packs, me_s, 1, False)[:, 2 * active : 2 * active + height]
    ranks = lax.dynamic_slice(ranks, (0, me_c * slots), (chan_count, slots)).astype(jnp.int32)
    signs_all = lax.dynamic_index_in_dim(packs, me_c, 0, False)[:, 2 * active + height :]
    hit = col_perm[0][:, None] == jnp.arange(breadth)[None, :]
    cc_inv = jnp.sum(jnp.where(hit, col_coef[0][:, None], 0.0), axis=0)
    order = (send_order[0][:, None] == jnp.arange(height)[None, :]).astype(BF16)
    return dict(
        cols=cols, act_cc=act_cc, ranks=ranks, signs_all=signs_all, cc_inv=cc_inv,
        order=order, act_rc=picked(row_coef[0]), act_sign=picked(sign), active=active,
    )


def on_device(omega, hamil, pp_sign, ph_sign, row_coef, col_coef, col_perm, send_order):
    chan_count = lax.axis_size("chan")
    _, height, breadth = omega.shape
    slots = height // chan_count
    me_c = lax.axis_index("chan")
    pre = prepare(omega, hamil, pp_sign, ph_sign, row_coef, col_coef, col_perm, send_order)
    active, order = pre["active"], pre["order"]
    omega_rows, hamil_rows = omega[0], hamil[0]

    scaled_h = (pp_sign[0][:, None] * hamil_rows).astype(BF16)
    all_h = lax.all_gather(scaled_h, "split", axis=0, tiled=True)

    sorted_o = dot(order, omega_rows).astype(BF16).reshape(chan_count, slots, breadth)
    sorted_h = dot(order, hamil_rows).astype(BF16).reshape(chan_count, slots, breadth)
    take = (pre["ranks"][:, None, :] == jnp.arange(active)[None, :, None]).astype(BF16)
    gate = (pre["cols"][:, None, :] == jnp.arange(breadth)[None, :, None]).astype(BF16)

    def batched(a, b):
        return jnp.einsum("qik,qkj->qij", a, b, preferred_element_type=F32).astype(BF16)

    parts = [batched(take, sorted_o), batched(take, sorted_h)]
    wide = pre["cols"].shape[1]
    left = jnp.concatenate([batched(sorted_o, gate), batched(sorted_h, gate)], axis=1)
    parts.append(left.reshape(chan_count, -1, breadth))
    sent = jnp.concatenate(parts, axis=1)
    got = lax.all_to_all(sent, "chan", split_axis=0, concat_axis=0, tiled=True)
    rows = jnp.sum(got[:, : 2 * active].astype(F32), axis=0)
    lefts = got[:, 2 * active :].reshape(chan_count, 2, slots, wide)
    coef_a = pre["act_rc"][:, None] * pre["cc_inv"][None, :]
    right_o = pre["act_sign"][:, None] * (coef_a * rows[:active]).astype(BF16).astype(F32)
    right_h = pre["act_sign"][:, None] * (coef_a * rows[active:]).astype(BF16).astype(F32)
    right = jnp.stack([right_h, right_o]).astype(BF16)
    rights = lax.all_gather(right, "split", axis=1, tiled=True)
    coef_l = row_coef[0][:, None] * pre["act_cc"][None, :]
    bar_o = (coef_l * lefts[:, 0].reshape(height, wide)).astype(BF16)
    bar_h = (coef_l * lefts[:, 1].reshape(height, wide)).astype(BF16)
    ph_sum = dot(jnp.concatenate([bar_o, -bar_h], axis=1), rights.reshape(-1, breadth))
    coefs = row_coef[0][:, None] * pre["cc_inv"][None, :]
    back = (coefs * ph_sum).astype(BF16)

    half = dot(omega_rows, all_h)
    flipped = lax.all_to_all(half.astype(BF16), "split", split_axis=1, concat_axis=0, tiled=True)

    returned = lax.all_to_all(
        back.reshape(chan_count, slots, breadth), "chan", split_axis=0, concat_axis=0, tiled=True
    )
    placed = lax.dot_general(
        order, returned.reshape(height, breadth), (((0,), (0,)), ((), ())),
        preferred_element_type=F32,
    )
    combined = half + flipped.T.astype(F32) + placed
    degeneracy = (2 * (me_c // 2) + 1).astype(F32)
    weight_sq = sum((2 * (i // 2) + 1) ** 2 for i in range(chan_count))
    local = degeneracy * jnp.sum(pp_sign[0][:, None] * combined, axis=0)
    one_body = lax.psum(local, ("chan", "split")) * (1.0 / math.sqrt(breadth * weight_sq))
    return combined.astype(BF16)[None], one_body


def solution(mesh):
    in_specs = (
        P("chan", "split", None),
        P("chan", "split", None),
        P("chan", "split"),
        P("chan", "split"),
        P("chan", "split"),
        P("chan", None),
        P("chan", None),
        P("chan", "split"),
    )
    out_specs = (P("chan", "split", None), P())
    return jax.shard_map(
        on_device, mesh=mesh, in_specs=in_specs, out_specs=out_specs, check_vma=False
    )
```

```python
import functools
import math

import jax
import jax.numpy as jnp
from jax import lax
from jax.experimental import pallas as pl
from jax.experimental.pallas import tpu as pltpu
from jax.sharding import PartitionSpec as P

F32, BF16 = jnp.float32, jnp.bfloat16


def dot(a, b):
    return jnp.dot(a, b, preferred_element_type=F32)


def prepare(omega, hamil, pp_sign, ph_sign, row_coef, col_coef, col_perm, send_order):
    chan_count = lax.axis_size("chan")
    _, height, breadth = omega.shape
    slots = height // chan_count
    active = height // 16
    me_c, me_s = lax.axis_index("chan"), lax.axis_index("split")
    sign = ph_sign[0]
    mask = sign != 0
    lower = jnp.arange(height)[:, None] <= jnp.arange(height)[None, :]
    rank = jnp.sum(jnp.where(lower & mask[:, None], 1, 0), axis=0) - 1
    rank = jnp.where(mask, rank, -1)
    pick = rank[None, :] == jnp.arange(active)[:, None]
    own_perm = lax.dynamic_slice(col_perm[0], (me_s * height,), (height,))
    own_cc = lax.dynamic_slice(col_coef[0], (me_s * height,), (height,))

    def picked(values):
        return jnp.sum(jnp.where(pick, values[None, :].astype(F32), 0.0), axis=1)

    pack = jnp.concatenate(
        [picked(own_perm), picked(own_cc), rank.astype(F32), pp_sign[0]]
    )
    packs = lax.all_gather(pack, ("chan", "split"), axis=0, tiled=False)
    packs = packs.reshape(chan_count, -1, pack.shape[0])
    cols = packs[:, :, :active].reshape(chan_count, -1).astype(jnp.int32)
    act_cc = lax.dynamic_index_in_dim(packs, me_c, 0, False)[:, active : 2 * active].reshape(-1)
    ranks = lax.dynamic_index_in_dim(packs, me_s, 1, False)[:, 2 * active : 2 * active + height]
    ranks = lax.dynamic_slice(ranks, (0, me_c * slots), (chan_count, slots)).astype(jnp.int32)
    signs_all = lax.dynamic_index_in_dim(packs, me_c, 0, False)[:, 2 * active + height :]
    hit = col_perm[0][:, None] == jnp.arange(breadth)[None, :]
    cc_inv = jnp.sum(jnp.where(hit, col_coef[0][:, None], 0.0), axis=0)
    order = (send_order[0][:, None] == jnp.arange(height)[None, :]).astype(BF16)
    return dict(
        cols=cols, act_cc=act_cc, ranks=ranks, signs_all=signs_all, cc_inv=cc_inv,
        order=order, act_rc=picked(row_coef[0]), act_sign=picked(sign), active=active,
    )


def on_device(omega, hamil, pp_sign, ph_sign, row_coef, col_coef, col_perm, send_order):
    chan_count = lax.axis_size("chan")
    _, height, breadth = omega.shape
    slots = height // chan_count
    me_c = lax.axis_index("chan")
    pre = prepare(omega, hamil, pp_sign, ph_sign, row_coef, col_coef, col_perm, send_order)
    active, order = pre["active"], pre["order"]
    omega_rows, hamil_rows = omega[0], hamil[0]

    scaled_h = (pp_sign[0][:, None] * hamil_rows).astype(BF16)
    all_h = lax.all_gather(scaled_h, "split", axis=0, tiled=True)

    sorted_o = dot(order, omega_rows).astype(BF16).reshape(chan_count, slots, breadth)
    sorted_h = dot(order, hamil_rows).astype(BF16).reshape(chan_count, slots, breadth)
    take = (pre["ranks"][:, None, :] == jnp.arange(active)[None, :, None]).astype(BF16)
    gate = (pre["cols"][:, None, :] == jnp.arange(breadth)[None, :, None]).astype(BF16)

    def batched(a, b):
        return jnp.einsum("qik,qkj->qij", a, b, preferred_element_type=F32).astype(BF16)

    parts = [batched(take, sorted_o), batched(take, sorted_h)]
    wide = pre["cols"].shape[1]
    left = jnp.concatenate([batched(sorted_o, gate), batched(sorted_h, gate)], axis=1)
    parts.append(left.reshape(chan_count, -1, breadth))
    sent = jnp.concatenate(parts, axis=1)
    got = lax.all_to_all(sent, "chan", split_axis=0, concat_axis=0, tiled=True)
    rows = jnp.sum(got[:, : 2 * active].astype(F32), axis=0)
    lefts = got[:, 2 * active :].reshape(chan_count, 2, slots, wide)
    coef_a = pre["act_rc"][:, None] * pre["cc_inv"][None, :]
    right_o = pre["act_sign"][:, None] * (coef_a * rows[:active]).astype(BF16).astype(F32)
    right_h = pre["act_sign"][:, None] * (coef_a * rows[active:]).astype(BF16).astype(F32)
    right = jnp.stack([right_h, right_o]).astype(BF16)
    rights = lax.all_gather(right, "split", axis=1, tiled=True)
    coef_l = row_coef[0][:, None] * pre["act_cc"][None, :]
    bar_o = (coef_l * lefts[:, 0].reshape(height, wide)).astype(BF16)
    bar_h = (coef_l * lefts[:, 1].reshape(height, wide)).astype(BF16)
    ph_sum = dot(jnp.concatenate([bar_o, -bar_h], axis=1), rights.reshape(-1, breadth))
    coefs = row_coef[0][:, None] * pre["cc_inv"][None, :]
    back = (coefs * ph_sum).astype(BF16)

    half = dot(omega_rows, all_h)
    flipped = lax.all_to_all(half.astype(BF16), "split", split_axis=1, concat_axis=0, tiled=True)

    returned = lax.all_to_all(
        back.reshape(chan_count, slots, breadth), "chan", split_axis=0, concat_axis=0, tiled=True
    )
    placed = lax.dot_general(
        order, returned.reshape(height, breadth), (((0,), (0,)), ((), ())),
        preferred_element_type=F32,
    )
    combined = half + flipped.T.astype(F32) + placed
    degeneracy = (2 * (me_c // 2) + 1).astype(F32)
    weight_sq = sum((2 * (i // 2) + 1) ** 2 for i in range(chan_count))
    local = degeneracy * jnp.sum(pp_sign[0][:, None] * combined, axis=0)
    one_body = lax.psum(local, ("chan", "split")) * (1.0 / math.sqrt(breadth * weight_sq))
    return combined.astype(BF16)[None], one_body


NT = (((1,), (1,)), ((), ()))


def fused(norm, omega, hamil, meta, ranks, cc_inv, colvec, actvec, order, order_t,
          z_out, ob_out,
          part_o, part_h, scal_o, scal_h, meta1, meta2s, meta2, sorted_r,
          send_a, recv_a, send_l, recv_l, ladder, x_send, x_recv, acc, rights,
          bars, back_s, back_r, ob1, ob2, right_s,
          p_send, p_recv, m1_send, m1_recv, m2_send, m2_recv, a_send, a_recv,
          l_send, l_recv, x_ss, x_rs, r_send, r_recv, b_send, b_recv,
          o1_send, o1_recv, o2_send, o2_recv):
    chans, splits = ob2.shape[0], ob1.shape[0]
    height, breadth = omega.shape
    slots = height // chans
    active = height // 16
    wide = active * splits
    c, s = lax.axis_index("chan"), lax.axis_index("split")
    partner = s + 1 - 2 * lax.rem(s, 2)
    far = 2 * (1 - s // 2)
    MESH = pl.DeviceIdType.MESH

    def remote(src, dst, ss, rs, cc, sp):
        return pltpu.make_async_remote_copy(
            src_ref=src, dst_ref=dst, send_sem=ss, recv_sem=rs,
            device_id=(cc, sp), device_id_type=MESH)

    def chan_loop(body):
        def step(d, carry):
            body(lax.rem(c + 1 + d, chans))
            return carry
        lax.fori_loop(0, chans - 1, step, 0)

    def split_loop(body):
        def step(d, carry):
            body(lax.rem(s + 1 + d, splits))
            return carry
        lax.fori_loop(0, splits - 1, step, 0)

    barrier = pltpu.get_barrier_semaphore()

    def greet(cc, sp):
        pl.semaphore_signal(barrier, inc=1, device_id=(cc, sp), device_id_type=MESH)

    chan_loop(lambda q: greet(q, s))
    split_loop(lambda p: greet(c, p))
    pl.semaphore_wait(barrier, chans + splits - 2)

    def m1(p, frm):
        return remote(meta, meta1.at[frm], m1_send.at[p], m1_recv.at[frm], c, p)
    split_loop(lambda p: m1(p, s).start())
    meta1[s] = meta[...]

    copy_o = remote(omega, part_o, p_send.at[0], p_recv.at[0], c, partner)
    copy_h = remote(hamil, part_h, p_send.at[1], p_recv.at[1], c, partner)
    copy_o.start()
    copy_h.start()

    tile = 256
    def sort_tile(n, carry):
        cols = pl.ds(pl.multiple_of(n * tile, tile), tile)
        got = dot(order[...], omega[:, cols]).astype(BF16)
        sorted_r[:, :slots, cols] = got.reshape(chans, slots, tile)
        got = dot(order[...], hamil[:, cols]).astype(BF16)
        sorted_r[:, slots:, cols] = got.reshape(chans, slots, tile)
        return carry
    lax.fori_loop(0, breadth // tile, sort_tile, 0)

    split_loop(lambda p: m1(p, p).wait_recv())
    sums = meta1[0] + meta1[1] + meta1[2] + meta1[3]
    cols_row, act_cc = sums[0:1, :wide], sums[1:2, :wide]
    for q in range(chans):
        meta2s[q] = ranks[q]
        meta2s[q, 0:1, :] = cols_row

    def m2(q, frm):
        return remote(meta2s.at[q], meta2.at[frm], m2_send.at[q], m2_recv.at[frm], q, s)
    chan_loop(lambda q: m2(q, c).start())
    meta2[c] = meta2s[c]

    def copy_a(q, frm):
        return remote(send_a.at[q], recv_a.at[frm], a_send.at[q], a_recv.at[frm], q, s)

    def copy_l(q, frm):
        return remote(send_l.at[q], recv_l.at[frm], l_send.at[q], l_recv.at[frm], q, s)

    def pack(q, rows_to, left_to):
        want = meta2[q]
        take = lax.broadcasted_iota(jnp.int32, (active, slots), 0).astype(F32)
        take = jnp.where(take == want[1:2, :slots], 1.0, 0.0).astype(BF16)
        rows_to[q, :active] = dot(take, sorted_r[q, :slots]).astype(BF16)
        rows_to[q, active:] = dot(take, sorted_r[q, slots:]).astype(BF16)
        gate = lax.broadcasted_iota(jnp.int32, (breadth, wide), 0).astype(F32)
        gate = jnp.where(gate == want[0:1, :wide], 1.0, 0.0).astype(BF16)
        left_to[q] = dot(sorted_r[q], gate).astype(BF16)

    def pack_send(q):
        m2(q, q).wait_recv()
        pack(q, send_a, send_l)
        copy_a(q, c).start()
        copy_l(q, c).start()
    chan_loop(pack_send)
    pack(c, recv_a, recv_l)

    span = height
    for k in range(splits):
        cols = slice(k * span, (k + 1) * span)
        sgn = meta1[k, 2:3, :]
        scal_o[:, cols] = (omega[:, cols].astype(F32) * sgn).astype(BF16)
        scal_h[:, cols] = (hamil[:, cols].astype(F32) * sgn).astype(BF16)
    copy_o.wait_recv()
    copy_h.wait_recv()
    own = pl.ds(pl.multiple_of(s * span, span), span)
    oth = pl.ds(pl.multiple_of(partner * span, span), span)

    def cross(m, carry):
        def half_tile(t, carry):
            cols = pl.ds(pl.multiple_of((far + m) * span + t * tile, tile), tile)
            val = dot(scal_o[:, own], hamil[:, cols]) - dot(scal_h[:, own], omega[:, cols])
            val = val + dot(scal_o[:, oth], part_h[:, cols]) - dot(scal_h[:, oth], part_o[:, cols])
            ladder[:, cols] = val
            x_send[m, :, pl.ds(pl.multiple_of(t * tile, tile), tile)] = val.astype(BF16)
            return carry
        return lax.fori_loop(0, span // tile, half_tile, carry)

    def copy_x(m, frm):
        return remote(x_send.at[m], x_recv.at[frm], x_ss.at[m], x_rs.at[frm], c, far + m)
    core = lax.rem(s, 2)
    for m in range(2):
        cross(m, 0)
        copy_x(m, core).start()

    def same(t, carry):
        rows = pl.ds(pl.multiple_of(t * tile, tile), tile)
        val = lax.dot_general(scal_o[...], part_h[rows], NT, preferred_element_type=F32)
        val = val + lax.dot_general(scal_h[...], part_o[rows], NT, preferred_element_type=F32)
        ladder[:, pl.ds(pl.multiple_of(partner * span + t * tile, tile), tile)] = val
        val = lax.dot_general(scal_o[...], hamil[rows], NT, preferred_element_type=F32)
        val = val + lax.dot_general(scal_h[...], omega[rows], NT, preferred_element_type=F32)
        ladder[:, pl.ds(pl.multiple_of(s * span + t * tile, tile), tile)] = val
        return carry
    lax.fori_loop(0, span // tile, same, 0)

    acc[...] = recv_a[c].astype(F32)

    def add_rows(q):
        copy_a(q, q).wait_recv()
        acc[...] += recv_a[q].astype(F32)
    chan_loop(add_rows)
    coef_a = actvec[:, 0:1] * cc_inv[...]
    signs = actvec[:, 1:2]
    right_s[1] = (-signs * (coef_a * acc[:active]).astype(BF16).astype(F32)).astype(BF16)
    right_s[0] = (signs * (coef_a * acc[active:]).astype(BF16).astype(F32)).astype(BF16)

    def place(p):
        return rights.at[:, pl.ds(pl.multiple_of(p * active, active), active), :]

    def copy_r(p, frm):
        return remote(right_s, place(frm), r_send.at[p], r_recv.at[frm], c, p)
    split_loop(lambda p: copy_r(p, s).start())
    rights[:, pl.ds(pl.multiple_of(s * active, active), active), :] = right_s[...]

    def make_bars(q):
        rows = pl.ds(pl.multiple_of(q * slots, slots), slots)
        coef = colvec[rows, 1:2] * act_cc
        bars[rows, :wide] = (coef * recv_l[q, :slots].astype(F32)).astype(BF16)
        bars[rows, wide:] = (coef * recv_l[q, slots:].astype(F32)).astype(BF16)

    def bars_from(q):
        copy_l(q, q).wait_recv()
        make_bars(q)
    chan_loop(bars_from)
    make_bars(c)
    split_loop(lambda p: copy_r(p, p).wait_recv())

    def copy_b(q, frm):
        return remote(back_s.at[q], back_r.at[frm], b_send.at[q], b_recv.at[frm], q, s)

    def product(q, to):
        rows = pl.ds(pl.multiple_of(q * slots, slots), slots)
        val = dot(bars[rows, :wide], rights[0]) + dot(bars[rows, wide:], rights[1])
        to[q] = (colvec[rows, 1:2] * cc_inv[...] * val).astype(BF16)

    def product_send(q):
        product(q, back_s)
        copy_b(q, c).start()
    chan_loop(product_send)
    product(c, back_r)

    for m in range(2):
        copy_x(m, m).wait_recv()
        def flip(t, carry):
            val = x_recv[m, :, pl.ds(pl.multiple_of(t * tile, tile), tile)]
            cols = pl.ds(pl.multiple_of((far + m) * span, span), span)
            ladder[pl.ds(pl.multiple_of(t * tile, tile), tile), cols] += val.astype(F32).T
            return carry
        lax.fori_loop(0, span // tile, flip, 0)

    chan_loop(lambda q: copy_b(q, q).wait_recv())

    degeneracy = (2 * (c // 2) + 1).astype(F32)
    weight = degeneracy * colvec[:, 0:1]

    def finish(n, carry):
        cols = pl.ds(pl.multiple_of(n * tile, tile), tile)
        total = ladder[:, cols] + dot(order_t[...], back_r[:, :, cols].reshape(height, tile))
        z_out[:, cols] = total.astype(BF16)
        ob1[s, pl.ds(n, 1), :] = jnp.sum(weight * total, axis=0, keepdims=True)
        return carry
    lax.fori_loop(0, breadth // tile, finish, 0)

    def copy_o1(p, frm):
        return remote(ob1.at[s], ob1.at[frm], o1_send.at[p], o1_recv.at[frm], c, p)
    split_loop(lambda p: copy_o1(p, s).start())
    split_loop(lambda p: copy_o1(p, p).wait_recv())
    ob2[c] = ob1[0] + ob1[1] + ob1[2] + ob1[3]

    def copy_o2(q, frm):
        return remote(ob2.at[c], ob2.at[frm], o2_send.at[q], o2_recv.at[frm], q, s)
    chan_loop(lambda q: copy_o2(q, c).start())
    chan_loop(lambda q: copy_o2(q, q).wait_recv())
    whole = ob2[0]
    for q in range(1, chans):
        whole = whole + ob2[q]
    ob_out[...] = whole * norm

    split_loop(lambda p: m1(p, s).wait_send())
    split_loop(lambda p: copy_r(p, s).wait_send())
    split_loop(lambda p: copy_o1(p, s).wait_send())
    copy_o.wait_send()
    copy_h.wait_send()
    for m in range(2):
        copy_x(m, core).wait_send()

    def sent(q):
        m2(q, c).wait_send()
        copy_a(q, c).wait_send()
        copy_l(q, c).wait_send()
        copy_b(q, c).wait_send()
        copy_o2(q, c).wait_send()
    chan_loop(sent)


def on_device_fused(omega, hamil, pp_sign, ph_sign, row_coef, col_coef, col_perm, send_order):
    chans, splits = lax.axis_size("chan"), lax.axis_size("split")
    _, height, breadth = omega.shape
    slots, active = height // chans, height // 16
    wide = active * splits
    me_s = lax.axis_index("split")
    sign = ph_sign[0]
    mask = sign != 0
    lower = jnp.arange(height)[:, None] <= jnp.arange(height)[None, :]
    rank = jnp.sum(jnp.where(lower & mask[:, None], 1, 0), axis=0) - 1
    rank = jnp.where(mask, rank, -1)
    own_perm = lax.dynamic_slice(col_perm[0], (me_s * height,), (height,)).astype(F32)
    own_cc = lax.dynamic_slice(col_coef[0], (me_s * height,), (height,))
    lanes = jnp.arange(height)
    pick = (rank[:, None] + me_s * active == lanes[None, :]) & mask[:, None]

    def picked(values):
        return jnp.sum(jnp.where(pick, values[:, None], 0.0), axis=0)
    pad = jnp.zeros((5, height), F32)
    meta = jnp.concatenate(
        [picked(own_perm)[None], picked(own_cc)[None], pp_sign[0][None], pad])
    ranks = jnp.pad(rank.astype(F32).reshape(chans, 1, slots),
                    ((0, 0), (1, 6), (0, wide - slots)), constant_values=-1.0)
    hit = col_perm[0][:, None] == jnp.arange(breadth)[None, :]
    cc_inv = jnp.sum(jnp.where(hit, col_coef[0][:, None], 0.0), axis=0)[None]
    colvec = jnp.stack([pp_sign[0], row_coef[0]], axis=1)
    colvec = jnp.pad(colvec, ((0, 0), (0, 126)))
    pick_a = rank[None, :] == jnp.arange(active)[:, None]
    actvec = jnp.stack([jnp.sum(jnp.where(pick_a, v[None, :], 0.0), axis=1)
                        for v in (row_coef[0], sign)], axis=1)
    actvec = jnp.pad(actvec, ((0, 0), (0, 126)))
    order = (send_order[0][:, None] == lanes[None, :]).astype(BF16)
    order_t = (send_order[0][None, :] == lanes[:, None]).astype(BF16)
    weight_sq = sum((2 * (i // 2) + 1) ** 2 for i in range(chans))
    norm = 1.0 / math.sqrt(breadth * weight_sq)
    vm = pl.BlockSpec(memory_space=pltpu.VMEM)
    dma = pltpu.SemaphoreType.DMA
    z_out, one_body = pl.pallas_call(
        functools.partial(fused, norm),
        out_shape=(jax.ShapeDtypeStruct((height, breadth), BF16),
                   jax.ShapeDtypeStruct((8, breadth // 8), F32)),
        in_specs=[vm] * 9,
        out_specs=(vm, vm),
        scratch_shapes=[
            pltpu.VMEM((height, breadth), BF16), pltpu.VMEM((height, breadth), BF16),
            pltpu.VMEM((height, breadth), BF16), pltpu.VMEM((height, breadth), BF16),
            pltpu.VMEM((splits, 8, height), F32),
            pltpu.VMEM((chans, 8, wide), F32), pltpu.VMEM((chans, 8, wide), F32),
            pltpu.VMEM((chans, 2 * slots, breadth), BF16),
            pltpu.VMEM((chans, 2 * active, breadth), BF16),
            pltpu.VMEM((chans, 2 * active, breadth), BF16),
            pltpu.VMEM((chans, 2 * slots, wide), BF16),
            pltpu.VMEM((chans, 2 * slots, wide), BF16),
            pltpu.VMEM((height, breadth), F32),
            pltpu.VMEM((2, height, height), BF16), pltpu.VMEM((2, height, height), BF16),
            pltpu.VMEM((2 * active, breadth), F32),
            pltpu.VMEM((2, wide, breadth), BF16),
            pltpu.VMEM((height, 2 * wide), BF16),
            pltpu.VMEM((chans, slots, breadth), BF16),
            pltpu.VMEM((chans, slots, breadth), BF16),
            pltpu.VMEM((splits, 8, breadth // 8), F32),
            pltpu.VMEM((chans, 8, breadth // 8), F32),
            pltpu.VMEM((2, active, breadth), BF16),
            dma((2,)), dma((2,)), dma((splits,)), dma((splits,)),
            dma((chans,)), dma((chans,)), dma((chans,)), dma((chans,)),
            dma((chans,)), dma((chans,)), dma((2,)), dma((2,)),
            dma((splits,)), dma((splits,)), dma((chans,)), dma((chans,)),
            dma((splits,)), dma((splits,)), dma((chans,)), dma((chans,)),
        ],
        compiler_params=pltpu.CompilerParams(
            collective_id=0, has_side_effects=True, vmem_limit_bytes=58 * 2**20),
    )(omega[0], hamil[0], meta, ranks, cc_inv, colvec, actvec, order, order_t)
    return z_out[None], one_body.reshape(-1)


def solution(mesh):
    small = mesh.shape["chan"] == 8 and mesh.shape["split"] == 4
    in_specs = (
        P("chan", "split", None),
        P("chan", "split", None),
        P("chan", "split"),
        P("chan", "split"),
        P("chan", "split"),
        P("chan", None),
        P("chan", None),
        P("chan", "split"),
    )
    out_specs = (P("chan", "split", None), P())
    return jax.shard_map(
        on_device_fused if small else on_device, mesh=mesh, in_specs=in_specs, out_specs=out_specs, check_vma=False
    )
```

```python
import functools
import math

import jax
import jax.numpy as jnp
from jax import lax
from jax.experimental import pallas as pl
from jax.experimental.pallas import tpu as pltpu
from jax.sharding import PartitionSpec as P

F32, BF16 = jnp.float32, jnp.bfloat16


def dot(a, b):
    return jnp.dot(a, b, preferred_element_type=F32)


def prepare(omega, hamil, pp_sign, ph_sign, row_coef, col_coef, col_perm, send_order):
    chan_count = lax.axis_size("chan")
    _, height, breadth = omega.shape
    slots = height // chan_count
    active = height // 16
    me_c, me_s = lax.axis_index("chan"), lax.axis_index("split")
    sign = ph_sign[0]
    mask = sign != 0
    lower = jnp.arange(height)[:, None] <= jnp.arange(height)[None, :]
    rank = jnp.sum(jnp.where(lower & mask[:, None], 1, 0), axis=0) - 1
    rank = jnp.where(mask, rank, -1)
    pick = rank[None, :] == jnp.arange(active)[:, None]
    own_perm = lax.dynamic_slice(col_perm[0], (me_s * height,), (height,))
    own_cc = lax.dynamic_slice(col_coef[0], (me_s * height,), (height,))

    def picked(values):
        return jnp.sum(jnp.where(pick, values[None, :].astype(F32), 0.0), axis=1)

    pack = jnp.concatenate(
        [picked(own_perm), picked(own_cc), rank.astype(F32), pp_sign[0]]
    )
    packs = lax.all_gather(pack, ("chan", "split"), axis=0, tiled=False)
    packs = packs.reshape(chan_count, -1, pack.shape[0])
    cols = packs[:, :, :active].reshape(chan_count, -1).astype(jnp.int32)
    act_cc = lax.dynamic_index_in_dim(packs, me_c, 0, False)[:, active : 2 * active].reshape(-1)
    ranks = lax.dynamic_index_in_dim(packs, me_s, 1, False)[:, 2 * active : 2 * active + height]
    ranks = lax.dynamic_slice(ranks, (0, me_c * slots), (chan_count, slots)).astype(jnp.int32)
    signs_all = lax.dynamic_index_in_dim(packs, me_c, 0, False)[:, 2 * active + height :]
    hit = col_perm[0][:, None] == jnp.arange(breadth)[None, :]
    cc_inv = jnp.sum(jnp.where(hit, col_coef[0][:, None], 0.0), axis=0)
    order = (send_order[0][:, None] == jnp.arange(height)[None, :]).astype(BF16)
    return dict(
        cols=cols, act_cc=act_cc, ranks=ranks, signs_all=signs_all, cc_inv=cc_inv,
        order=order, act_rc=picked(row_coef[0]), act_sign=picked(sign), active=active,
    )


def on_device(omega, hamil, pp_sign, ph_sign, row_coef, col_coef, col_perm, send_order):
    chan_count = lax.axis_size("chan")
    _, height, breadth = omega.shape
    slots = height // chan_count
    me_c = lax.axis_index("chan")
    pre = prepare(omega, hamil, pp_sign, ph_sign, row_coef, col_coef, col_perm, send_order)
    active, order = pre["active"], pre["order"]
    omega_rows, hamil_rows = omega[0], hamil[0]

    scaled_h = (pp_sign[0][:, None] * hamil_rows).astype(BF16)
    all_h = lax.all_gather(scaled_h, "split", axis=0, tiled=True)

    sorted_o = dot(order, omega_rows).astype(BF16).reshape(chan_count, slots, breadth)
    sorted_h = dot(order, hamil_rows).astype(BF16).reshape(chan_count, slots, breadth)
    take = (pre["ranks"][:, None, :] == jnp.arange(active)[None, :, None]).astype(BF16)
    gate = (pre["cols"][:, None, :] == jnp.arange(breadth)[None, :, None]).astype(BF16)

    def batched(a, b):
        return jnp.einsum("qik,qkj->qij", a, b, preferred_element_type=F32).astype(BF16)

    parts = [batched(take, sorted_o), batched(take, sorted_h)]
    wide = pre["cols"].shape[1]
    left = jnp.concatenate([batched(sorted_o, gate), batched(sorted_h, gate)], axis=1)
    parts.append(left.reshape(chan_count, -1, breadth))
    sent = jnp.concatenate(parts, axis=1)
    got = lax.all_to_all(sent, "chan", split_axis=0, concat_axis=0, tiled=True)
    rows = jnp.sum(got[:, : 2 * active].astype(F32), axis=0)
    lefts = got[:, 2 * active :].reshape(chan_count, 2, slots, wide)
    coef_a = pre["act_rc"][:, None] * pre["cc_inv"][None, :]
    right_o = pre["act_sign"][:, None] * (coef_a * rows[:active]).astype(BF16).astype(F32)
    right_h = pre["act_sign"][:, None] * (coef_a * rows[active:]).astype(BF16).astype(F32)
    right = jnp.stack([right_h, right_o]).astype(BF16)
    rights = lax.all_gather(right, "split", axis=1, tiled=True)
    coef_l = row_coef[0][:, None] * pre["act_cc"][None, :]
    bar_o = (coef_l * lefts[:, 0].reshape(height, wide)).astype(BF16)
    bar_h = (coef_l * lefts[:, 1].reshape(height, wide)).astype(BF16)
    ph_sum = dot(jnp.concatenate([bar_o, -bar_h], axis=1), rights.reshape(-1, breadth))
    coefs = row_coef[0][:, None] * pre["cc_inv"][None, :]
    back = (coefs * ph_sum).astype(BF16)

    half = dot(omega_rows, all_h)
    flipped = lax.all_to_all(half.astype(BF16), "split", split_axis=1, concat_axis=0, tiled=True)

    returned = lax.all_to_all(
        back.reshape(chan_count, slots, breadth), "chan", split_axis=0, concat_axis=0, tiled=True
    )
    placed = lax.dot_general(
        order, returned.reshape(height, breadth), (((0,), (0,)), ((), ())),
        preferred_element_type=F32,
    )
    combined = half + flipped.T.astype(F32) + placed
    degeneracy = (2 * (me_c // 2) + 1).astype(F32)
    weight_sq = sum((2 * (i // 2) + 1) ** 2 for i in range(chan_count))
    local = degeneracy * jnp.sum(pp_sign[0][:, None] * combined, axis=0)
    one_body = lax.psum(local, ("chan", "split")) * (1.0 / math.sqrt(breadth * weight_sq))
    return combined.astype(BF16)[None], one_body


NT = (((1,), (1,)), ((), ()))


def fused(norm, omega, hamil, pp, phs, rcr, ccr, permr, sor,
          z_out, ob_out,
          part_o, part_h, scal_o, scal_h, meta1, meta2s, meta2, sorted_r,
          send_a, recv_a, send_l, recv_l, ladder, x_send, x_recv, acc, rights,
          bars, back_s, back_r, ob1, ob2, right_s,
          send_y, recv_y, meta, cc_parts, cc_inv, colvec, order, order_t,
          p_send, p_recv, m1_send, m1_recv, m2_send, m2_recv, a_send, a_recv,
          l_send, l_recv, x_ss, x_rs, r_send, r_recv, b_send, b_recv,
          o1_send, o1_recv, o2_send, o2_recv, y_send, y_recv):
    chans, splits = ob2.shape[0], ob1.shape[0]
    height, breadth = omega.shape
    slots = height // chans
    active = height // 16
    wide = active * splits
    c, s = lax.axis_index("chan"), lax.axis_index("split")
    partner = s + 1 - 2 * lax.rem(s, 2)
    far = 2 * (1 - s // 2)
    MESH = pl.DeviceIdType.MESH

    def remote(src, dst, ss, rs, cc, sp):
        return pltpu.make_async_remote_copy(
            src_ref=src, dst_ref=dst, send_sem=ss, recv_sem=rs,
            device_id=(cc, sp), device_id_type=MESH)

    def chan_loop(body):
        def step(d, carry):
            body(lax.rem(c + 1 + d, chans))
            return carry
        lax.fori_loop(0, chans - 1, step, 0)

    def split_loop(body):
        def step(d, carry):
            body(lax.rem(s + 1 + d, splits))
            return carry
        lax.fori_loop(0, splits - 1, step, 0)

    barrier = pltpu.get_barrier_semaphore()

    def greet(cc, sp):
        pl.semaphore_signal(barrier, inc=1, device_id=(cc, sp), device_id_type=MESH)

    chan_loop(lambda q: greet(q, s))
    split_loop(lambda p: greet(c, p))
    pl.semaphore_wait(barrier, chans + splits - 2)

    copy_o = remote(omega, part_o, p_send.at[0], p_recv.at[0], c, partner)
    copy_h = remote(hamil, part_h, p_send.at[1], p_recv.at[1], c, partner)
    copy_o.start()
    copy_h.start()

    own_cols = pl.ds(pl.multiple_of(s * height, height), height)
    down = lax.broadcasted_iota(jnp.int32, (height, height), 0)
    over = lax.broadcasted_iota(jnp.int32, (height, height), 1)
    mask = jnp.where(phs[...] != 0.0, 1.0, 0.0)
    lower = jnp.where(down <= over, 1.0, 0.0).astype(BF16)
    count = dot(jnp.broadcast_to(mask, (16, height)).astype(BF16), lower)[0:1]
    rank = jnp.where(mask > 0.0, count - 1.0, -1.0)
    lane_of = jnp.where(mask > 0.0, count - 1.0 + (s * active).astype(F32), -1.0)
    pick = lax.broadcasted_iota(jnp.int32, (wide, height), 0).astype(F32)
    pick = jnp.where(pick == lane_of, 1.0, 0.0)
    meta[...] = jnp.zeros_like(meta)
    meta[0:1, :] = permr[:, own_cols].astype(F32)
    meta[1:2, :] = ccr[:, own_cols]
    chosen = lax.dot_general(meta[...], pick, NT, precision=lax.Precision.HIGHEST,
                             preferred_element_type=F32)
    meta[0:2, :wide] = chosen[0:2]
    meta[2:3, :] = pp[...]

    def m1(p, frm):
        return remote(meta, meta1.at[frm], m1_send.at[p], m1_recv.at[frm], c, p)
    split_loop(lambda p: m1(p, s).start())
    meta1[s] = meta[...]

    turned = jnp.where(down == sor[...], 1.0, 0.0)
    order_t[...] = turned.astype(BF16)
    order[...] = turned.T.astype(BF16)
    colvec[:, 0:1] = jnp.sum(jnp.where(down == over, pp[...], 0.0), axis=1, keepdims=True)
    colvec[:, 1:2] = jnp.sum(jnp.where(down == over, rcr[...], 0.0), axis=1, keepdims=True)

    tile = 256
    def sort_tile(n, carry):
        cols = pl.ds(pl.multiple_of(n * tile, tile), tile)
        got = dot(order[...], omega[:, cols]).astype(BF16)
        sorted_r[:, :slots, cols] = got.reshape(chans, slots, tile)
        got = dot(order[...], hamil[:, cols]).astype(BF16)
        sorted_r[:, slots:, cols] = got.reshape(chans, slots, tile)
        return carry
    lax.fori_loop(0, breadth // tile, sort_tile, 0)

    split_loop(lambda p: m1(p, p).wait_recv())
    sums = meta1[0] + meta1[1] + meta1[2] + meta1[3]
    cols_row, act_cc = sums[0:1, :wide], sums[1:2, :wide]
    for q in range(chans):
        meta2s[q] = jnp.zeros(meta2s.shape[1:], F32)
        meta2s[q, 1:2, :slots] = rank[:, q * slots : (q + 1) * slots]
        meta2s[q, 0:1, :] = cols_row

    def m2(q, frm):
        return remote(meta2s.at[q], meta2.at[frm], m2_send.at[q], m2_recv.at[frm], q, s)
    chan_loop(lambda q: m2(q, c).start())
    meta2[c] = meta2s[c]

    rungs = chans // 2
    z, y = c // 2, lax.rem(c, 2)

    def copy_y(to):
        return remote(send_y.at[to], recv_y.at[to], y_send.at[to], y_recv.at[to],
                      z * 2 + 1 - y, s)

    def copy_a(to, frm):
        return remote(send_a.at[to], recv_a.at[frm], a_send.at[to], a_recv.at[frm],
                      to * 2 + y, s)

    def copy_l(q, frm):
        return remote(send_l.at[q], recv_l.at[frm], l_send.at[q], l_recv.at[frm], q, s)

    def pack_rows(q):
        take = lax.broadcasted_iota(jnp.int32, (active, slots), 0).astype(F32)
        take = jnp.where(take == meta2[q, 1:2, :slots], 1.0, 0.0).astype(BF16)
        return dot(take, sorted_r[q, :slots]), dot(take, sorted_r[q, slots:])

    def pack_left(q, to):
        gate = lax.broadcasted_iota(jnp.int32, (breadth, wide), 0).astype(F32)
        gate = jnp.where(gate == meta2[q, 0:1, :wide], 1.0, 0.0).astype(BF16)
        to[q] = dot(sorted_r[q], gate).astype(BF16)

    def to_side(d, carry):
        to = lax.rem(z + 1 + d, rungs)
        q = to * 2 + 1 - y
        m2(q, q).wait_recv()
        got_o, got_h = pack_rows(q)
        send_y[to, :active] = got_o.astype(BF16)
        send_y[to, active:] = got_h.astype(BF16)
        copy_y(to).start()
        return carry
    lax.fori_loop(0, rungs, to_side, 0)

    def along(to, out):
        got_o, got_h = pack_rows(to * 2 + y)
        copy_y(to).wait_recv()
        out[to, :active] = (got_o + recv_y[to, :active].astype(F32)).astype(BF16)
        out[to, active:] = (got_h + recv_y[to, active:].astype(F32)).astype(BF16)

    def along_send(d, carry):
        to = lax.rem(z + 1 + d, rungs)
        m2(to * 2 + y, to * 2 + y).wait_recv()
        along(to, send_a)
        copy_a(to, z).start()
        return carry
    lax.fori_loop(0, rungs - 1, along_send, 0)

    def left_send(q):
        pack_left(q, send_l)
        copy_l(q, c).start()
    chan_loop(left_send)
    pack_left(c, recv_l)
    along(z, recv_a)

    span = height
    for k in range(splits):
        cols = slice(k * span, (k + 1) * span)
        sgn = meta1[k, 2:3, :]
        scal_o[:, cols] = (omega[:, cols].astype(F32) * sgn).astype(BF16)
        scal_h[:, cols] = (hamil[:, cols].astype(F32) * sgn).astype(BF16)
    copy_o.wait_recv()
    copy_h.wait_recv()
    own = pl.ds(pl.multiple_of(s * span, span), span)
    oth = pl.ds(pl.multiple_of(partner * span, span), span)

    def cross(m, carry):
        def half_tile(t, carry):
            cols = pl.ds(pl.multiple_of((far + m) * span + t * tile, tile), tile)
            val = dot(scal_o[:, own], hamil[:, cols]) - dot(scal_h[:, own], omega[:, cols])
            val = val + dot(scal_o[:, oth], part_h[:, cols]) - dot(scal_h[:, oth], part_o[:, cols])
            ladder[:, cols] = val
            x_send[m, :, pl.ds(pl.multiple_of(t * tile, tile), tile)] = val.astype(BF16)
            return carry
        return lax.fori_loop(0, span // tile, half_tile, carry)

    def copy_x(m, frm):
        return remote(x_send.at[m], x_recv.at[frm], x_ss.at[m], x_rs.at[frm], c, far + m)
    core = lax.rem(s, 2)
    for m in range(2):
        cross(m, 0)
        copy_x(m, core).start()

    def same(t, carry):
        rows = pl.ds(pl.multiple_of(t * tile, tile), tile)
        val = lax.dot_general(scal_o[...], part_h[rows], NT, preferred_element_type=F32)
        val = val + lax.dot_general(scal_h[...], part_o[rows], NT, preferred_element_type=F32)
        ladder[:, pl.ds(pl.multiple_of(partner * span + t * tile, tile), tile)] = val
        val = lax.dot_general(scal_o[...], hamil[rows], NT, preferred_element_type=F32)
        val = val + lax.dot_general(scal_h[...], omega[rows], NT, preferred_element_type=F32)
        ladder[:, pl.ds(pl.multiple_of(s * span + t * tile, tile), tile)] = val
        return carry
    lax.fori_loop(0, span // tile, same, 0)

    cc_parts[...] = jnp.zeros_like(cc_parts)
    first = ccr[...].astype(BF16).astype(F32)
    second = (ccr[...] - first).astype(BF16).astype(F32)
    third = ccr[...] - first - second
    cc_parts[0:1, :] = first
    cc_parts[1:2, :] = second
    cc_parts[2:3, :] = third

    def invert(n, carry):
        hit = lax.broadcasted_iota(jnp.int32, (tile, breadth), 0) + n * tile
        hit = jnp.where(hit == permr[...], 1.0, 0.0).astype(BF16)
        val = lax.dot_general(cc_parts[...].astype(BF16), hit, NT, preferred_element_type=F32)
        cc_inv[:, pl.ds(pl.multiple_of(n * tile, tile), tile)] = jnp.sum(
            val, axis=0, keepdims=True)
        return carry
    lax.fori_loop(0, breadth // tile, invert, 0)
    slot_of = lax.broadcasted_iota(jnp.int32, (active, height), 0).astype(F32)
    act_rc = jnp.sum(jnp.where(slot_of == rank, rcr[...], 0.0), axis=1, keepdims=True)
    signs = jnp.sum(jnp.where(slot_of == rank, phs[...], 0.0), axis=1, keepdims=True)

    acc[...] = recv_a[z].astype(F32)

    def add_rows(d, carry):
        frm = lax.rem(z + 1 + d, rungs)
        copy_a(frm, frm).wait_recv()
        acc[...] += recv_a[frm].astype(F32)
        return carry
    lax.fori_loop(0, rungs - 1, add_rows, 0)
    coef_a = act_rc * cc_inv[...]
    right_s[1] = (-signs * (coef_a * acc[:active]).astype(BF16).astype(F32)).astype(BF16)
    right_s[0] = (signs * (coef_a * acc[active:]).astype(BF16).astype(F32)).astype(BF16)

    def place(p):
        return rights.at[:, pl.ds(pl.multiple_of(p * active, active), active), :]

    away = lax.rem(s + 2, splits)
    partner_away = lax.rem(partner + 2, splits)

    def copy_r(src, block, p, which):
        return remote(src, place(block), r_send.at[which], r_recv.at[block], c, p)
    copy_r(right_s, s, away, 0).start()
    copy_r(right_s, s, partner, 1).start()
    rights[:, pl.ds(pl.multiple_of(s * active, active), active), :] = right_s[...]

    def make_bars(q):
        rows = pl.ds(pl.multiple_of(q * slots, slots), slots)
        coef = colvec[rows, 1:2] * act_cc
        bars[rows, :wide] = (coef * recv_l[q, :slots].astype(F32)).astype(BF16)
        bars[rows, wide:] = (coef * recv_l[q, slots:].astype(F32)).astype(BF16)

    def bars_from(q):
        copy_l(q, q).wait_recv()
        make_bars(q)
    chan_loop(bars_from)
    make_bars(c)
    copy_r(right_s, away, away, 0).wait_recv()
    copy_r(place(away), away, partner, 2).start()
    copy_r(right_s, partner, partner, 1).wait_recv()
    copy_r(right_s, partner_away, partner, 2).wait_recv()

    def copy_b(q, frm):
        return remote(back_s.at[q], back_r.at[frm], b_send.at[q], b_recv.at[frm], q, s)

    def product(q, to):
        rows = pl.ds(pl.multiple_of(q * slots, slots), slots)
        val = dot(bars[rows, :wide], rights[0]) + dot(bars[rows, wide:], rights[1])
        to[q] = (colvec[rows, 1:2] * cc_inv[...] * val).astype(BF16)

    def product_send(q):
        product(q, back_s)
        copy_b(q, c).start()
    chan_loop(product_send)
    product(c, back_r)

    for m in range(2):
        copy_x(m, m).wait_recv()
        def flip(t, carry):
            val = x_recv[m, :, pl.ds(pl.multiple_of(t * tile, tile), tile)]
            cols = pl.ds(pl.multiple_of((far + m) * span, span), span)
            ladder[pl.ds(pl.multiple_of(t * tile, tile), tile), cols] += val.astype(F32).T
            return carry
        lax.fori_loop(0, span // tile, flip, 0)

    chan_loop(lambda q: copy_b(q, q).wait_recv())

    degeneracy = (2 * (c // 2) + 1).astype(F32)
    weight = degeneracy * colvec[:, 0:1]

    def finish(n, carry):
        cols = pl.ds(pl.multiple_of(n * tile, tile), tile)
        total = ladder[:, cols] + dot(order_t[...], back_r[:, :, cols].reshape(height, tile))
        z_out[:, cols] = total.astype(BF16)
        ob1[s, pl.ds(n, 1), :] = jnp.sum(weight * total, axis=0, keepdims=True)
        return carry
    lax.fori_loop(0, breadth // tile, finish, 0)

    def copy_o1(p, frm):
        return remote(ob1.at[s], ob1.at[frm], o1_send.at[p], o1_recv.at[frm], c, p)
    split_loop(lambda p: copy_o1(p, s).start())
    split_loop(lambda p: copy_o1(p, p).wait_recv())
    ob2[c] = ob1[0] + ob1[1] + ob1[2] + ob1[3]

    def copy_o2(q, frm):
        return remote(ob2.at[c], ob2.at[frm], o2_send.at[q], o2_recv.at[frm], q, s)
    chan_loop(lambda q: copy_o2(q, c).start())
    chan_loop(lambda q: copy_o2(q, q).wait_recv())
    whole = ob2[0]
    for q in range(1, chans):
        whole = whole + ob2[q]
    ob_out[...] = whole * norm

    split_loop(lambda p: m1(p, s).wait_send())
    copy_r(right_s, s, away, 0).wait_send()
    copy_r(right_s, s, partner, 1).wait_send()
    copy_r(place(away), away, partner, 2).wait_send()
    split_loop(lambda p: copy_o1(p, s).wait_send())
    copy_o.wait_send()
    copy_h.wait_send()
    for m in range(2):
        copy_x(m, core).wait_send()

    def sent(q):
        m2(q, c).wait_send()
        copy_l(q, c).wait_send()
        copy_b(q, c).wait_send()
        copy_o2(q, c).wait_send()
    chan_loop(sent)

    def sent_rows(d, carry):
        copy_a(lax.rem(z + 1 + d, rungs), z).wait_send()
        return carry
    lax.fori_loop(0, rungs - 1, sent_rows, 0)

    def sent_side(d, carry):
        copy_y(d).wait_send()
        return carry
    lax.fori_loop(0, rungs, sent_side, 0)


def on_device_fused(omega, hamil, pp_sign, ph_sign, row_coef, col_coef, col_perm, send_order):
    chans, splits = lax.axis_size("chan"), lax.axis_size("split")
    _, height, breadth = omega.shape
    slots, active = height // chans, height // 16
    wide = active * splits
    rungs = chans // 2
    weight_sq = sum((2 * (i // 2) + 1) ** 2 for i in range(chans))
    norm = 1.0 / math.sqrt(breadth * weight_sq)
    vm = pl.BlockSpec(memory_space=pltpu.VMEM)
    dma = pltpu.SemaphoreType.DMA
    z_out, one_body = pl.pallas_call(
        functools.partial(fused, norm),
        out_shape=(jax.ShapeDtypeStruct((height, breadth), BF16),
                   jax.ShapeDtypeStruct((8, breadth // 8), F32)),
        in_specs=[vm] * 8,
        out_specs=(vm, vm),
        scratch_shapes=[
            pltpu.VMEM((height, breadth), BF16), pltpu.VMEM((height, breadth), BF16),
            pltpu.VMEM((height, breadth), BF16), pltpu.VMEM((height, breadth), BF16),
            pltpu.VMEM((splits, 8, height), F32),
            pltpu.VMEM((chans, 8, wide), F32), pltpu.VMEM((chans, 8, wide), F32),
            pltpu.VMEM((chans, 2 * slots, breadth), BF16),
            pltpu.VMEM((rungs, 2 * active, breadth), BF16),
            pltpu.VMEM((rungs, 2 * active, breadth), BF16),
            pltpu.VMEM((chans, 2 * slots, wide), BF16),
            pltpu.VMEM((chans, 2 * slots, wide), BF16),
            pltpu.VMEM((height, breadth), F32),
            pltpu.VMEM((2, height, height), BF16), pltpu.VMEM((2, height, height), BF16),
            pltpu.VMEM((2 * active, breadth), F32),
            pltpu.VMEM((2, wide, breadth), BF16),
            pltpu.VMEM((height, 2 * wide), BF16),
            pltpu.VMEM((chans, slots, breadth), BF16),
            pltpu.VMEM((chans, slots, breadth), BF16),
            pltpu.VMEM((splits, 8, breadth // 8), F32),
            pltpu.VMEM((chans, 8, breadth // 8), F32),
            pltpu.VMEM((2, active, breadth), BF16),
            pltpu.VMEM((rungs, 2 * active, breadth), BF16),
            pltpu.VMEM((rungs, 2 * active, breadth), BF16),
            pltpu.VMEM((8, height), F32),
            pltpu.VMEM((16, breadth), F32),
            pltpu.VMEM((1, breadth), F32),
            pltpu.VMEM((height, 128), F32),
            pltpu.VMEM((height, height), BF16), pltpu.VMEM((height, height), BF16),
            dma((2,)), dma((2,)), dma((splits,)), dma((splits,)),
            dma((chans,)), dma((chans,)), dma((chans,)), dma((chans,)),
            dma((chans,)), dma((chans,)), dma((2,)), dma((2,)),
            dma((splits,)), dma((splits,)), dma((chans,)), dma((chans,)),
            dma((splits,)), dma((splits,)), dma((chans,)), dma((chans,)),
            dma((rungs,)), dma((rungs,)),
        ],
        compiler_params=pltpu.CompilerParams(
            collective_id=0, has_side_effects=True, vmem_limit_bytes=58 * 2**20),
    )(omega[0], hamil[0], pp_sign, ph_sign, row_coef, col_coef, col_perm, send_order)
    return z_out[None], one_body.reshape(-1)


def solution(mesh):
    small = mesh.shape["chan"] == 8 and mesh.shape["split"] == 4
    in_specs = (
        P("chan", "split", None),
        P("chan", "split", None),
        P("chan", "split"),
        P("chan", "split"),
        P("chan", "split"),
        P("chan", None),
        P("chan", None),
        P("chan", "split"),
    )
    out_specs = (P("chan", "split", None), P())
    return jax.shard_map(
        on_device_fused if small else on_device, mesh=mesh, in_specs=in_specs, out_specs=out_specs, check_vma=False
    )
```

```python
import functools
import math

import jax
import jax.numpy as jnp
from jax import lax
from jax.experimental import pallas as pl
from jax.experimental.pallas import tpu as pltpu
from jax.sharding import PartitionSpec as P

F32, BF16 = jnp.float32, jnp.bfloat16


def dot(a, b):
    return jnp.dot(a, b, preferred_element_type=F32)


def prepare(omega, hamil, pp_sign, ph_sign, row_coef, col_coef, col_perm, send_order):
    chan_count = lax.axis_size("chan")
    _, height, breadth = omega.shape
    slots = height // chan_count
    active = height // 16
    me_c, me_s = lax.axis_index("chan"), lax.axis_index("split")
    sign = ph_sign[0]
    mask = sign != 0
    lower = jnp.arange(height)[:, None] <= jnp.arange(height)[None, :]
    rank = jnp.sum(jnp.where(lower & mask[:, None], 1, 0), axis=0) - 1
    rank = jnp.where(mask, rank, -1)
    pick = rank[None, :] == jnp.arange(active)[:, None]
    own_perm = lax.dynamic_slice(col_perm[0], (me_s * height,), (height,))
    own_cc = lax.dynamic_slice(col_coef[0], (me_s * height,), (height,))

    def picked(values):
        return jnp.sum(jnp.where(pick, values[None, :].astype(F32), 0.0), axis=1)

    pack = jnp.concatenate(
        [picked(own_perm), picked(own_cc), rank.astype(F32), pp_sign[0]]
    )
    packs = lax.all_gather(pack, ("chan", "split"), axis=0, tiled=False)
    packs = packs.reshape(chan_count, -1, pack.shape[0])
    cols = packs[:, :, :active].reshape(chan_count, -1).astype(jnp.int32)
    act_cc = lax.dynamic_index_in_dim(packs, me_c, 0, False)[:, active : 2 * active].reshape(-1)
    ranks = lax.dynamic_index_in_dim(packs, me_s, 1, False)[:, 2 * active : 2 * active + height]
    ranks = lax.dynamic_slice(ranks, (0, me_c * slots), (chan_count, slots)).astype(jnp.int32)
    signs_all = lax.dynamic_index_in_dim(packs, me_c, 0, False)[:, 2 * active + height :]
    hit = col_perm[0][:, None] == jnp.arange(breadth)[None, :]
    cc_inv = jnp.sum(jnp.where(hit, col_coef[0][:, None], 0.0), axis=0)
    order = (send_order[0][:, None] == jnp.arange(height)[None, :]).astype(BF16)
    return dict(
        cols=cols, act_cc=act_cc, ranks=ranks, signs_all=signs_all, cc_inv=cc_inv,
        order=order, act_rc=picked(row_coef[0]), act_sign=picked(sign), active=active,
    )


def on_device(omega, hamil, pp_sign, ph_sign, row_coef, col_coef, col_perm, send_order):
    chan_count = lax.axis_size("chan")
    _, height, breadth = omega.shape
    slots = height // chan_count
    me_c = lax.axis_index("chan")
    pre = prepare(omega, hamil, pp_sign, ph_sign, row_coef, col_coef, col_perm, send_order)
    active, order = pre["active"], pre["order"]
    omega_rows, hamil_rows = omega[0], hamil[0]

    scaled_h = (pp_sign[0][:, None] * hamil_rows).astype(BF16)
    all_h = lax.all_gather(scaled_h, "split", axis=0, tiled=True)

    sorted_o = dot(order, omega_rows).astype(BF16).reshape(chan_count, slots, breadth)
    sorted_h = dot(order, hamil_rows).astype(BF16).reshape(chan_count, slots, breadth)
    take = (pre["ranks"][:, None, :] == jnp.arange(active)[None, :, None]).astype(BF16)
    gate = (pre["cols"][:, None, :] == jnp.arange(breadth)[None, :, None]).astype(BF16)

    def batched(a, b):
        return jnp.einsum("qik,qkj->qij", a, b, preferred_element_type=F32).astype(BF16)

    parts = [batched(take, sorted_o), batched(take, sorted_h)]
    wide = pre["cols"].shape[1]
    left = jnp.concatenate([batched(sorted_o, gate), batched(sorted_h, gate)], axis=1)
    parts.append(left.reshape(chan_count, -1, breadth))
    sent = jnp.concatenate(parts, axis=1)
    got = lax.all_to_all(sent, "chan", split_axis=0, concat_axis=0, tiled=True)
    rows = jnp.sum(got[:, : 2 * active].astype(F32), axis=0)
    lefts = got[:, 2 * active :].reshape(chan_count, 2, slots, wide)
    coef_a = pre["act_rc"][:, None] * pre["cc_inv"][None, :]
    right_o = pre["act_sign"][:, None] * (coef_a * rows[:active]).astype(BF16).astype(F32)
    right_h = pre["act_sign"][:, None] * (coef_a * rows[active:]).astype(BF16).astype(F32)
    right = jnp.stack([right_h, right_o]).astype(BF16)
    rights = lax.all_gather(right, "split", axis=1, tiled=True)
    coef_l = row_coef[0][:, None] * pre["act_cc"][None, :]
    bar_o = (coef_l * lefts[:, 0].reshape(height, wide)).astype(BF16)
    bar_h = (coef_l * lefts[:, 1].reshape(height, wide)).astype(BF16)
    ph_sum = dot(jnp.concatenate([bar_o, -bar_h], axis=1), rights.reshape(-1, breadth))
    coefs = row_coef[0][:, None] * pre["cc_inv"][None, :]
    back = (coefs * ph_sum).astype(BF16)

    half = dot(omega_rows, all_h)
    flipped = lax.all_to_all(half.astype(BF16), "split", split_axis=1, concat_axis=0, tiled=True)

    returned = lax.all_to_all(
        back.reshape(chan_count, slots, breadth), "chan", split_axis=0, concat_axis=0, tiled=True
    )
    placed = lax.dot_general(
        order, returned.reshape(height, breadth), (((0,), (0,)), ((), ())),
        preferred_element_type=F32,
    )
    combined = half + flipped.T.astype(F32) + placed
    degeneracy = (2 * (me_c // 2) + 1).astype(F32)
    weight_sq = sum((2 * (i // 2) + 1) ** 2 for i in range(chan_count))
    local = degeneracy * jnp.sum(pp_sign[0][:, None] * combined, axis=0)
    one_body = lax.psum(local, ("chan", "split")) * (1.0 / math.sqrt(breadth * weight_sq))
    return combined.astype(BF16)[None], one_body


NT = (((1,), (1,)), ((), ()))


def fused(norm, omega, hamil, pp, phs, rcr, ccr, permr, sor,
          z_out, ob_out,
          part_o, part_h, scal_o, scal_h, meta1, meta2s, meta2, sorted_r,
          send_a, recv_a, send_l, recv_l, ladder, x_send, x_recv, acc, rights,
          bars, back_s, back_r, ob1, ob2, right_s,
          send_y, recv_y, meta, cc_parts, cc_inv, colvec, order, order_t,
          p_send, p_recv, m1_send, m1_recv, m2_send, m2_recv, a_send, a_recv,
          l_send, l_recv, x_ss, x_rs, r_send, r_recv, b_send, b_recv,
          o1_send, o1_recv, o2_send, o2_recv, y_send, y_recv):
    chans, splits = ob2.shape[0], ob1.shape[0]
    height, breadth = omega.shape
    slots = height // chans
    active = height // 16
    wide = active * splits
    c, s = lax.axis_index("chan"), lax.axis_index("split")
    partner = s + 1 - 2 * lax.rem(s, 2)
    far = 2 * (1 - s // 2)
    MESH = pl.DeviceIdType.MESH

    def remote(src, dst, ss, rs, cc, sp):
        return pltpu.make_async_remote_copy(
            src_ref=src, dst_ref=dst, send_sem=ss, recv_sem=rs,
            device_id=(cc, sp), device_id_type=MESH)

    def chan_loop(body):
        def step(d, carry):
            body(lax.rem(c + 1 + d, chans))
            return carry
        lax.fori_loop(0, chans - 1, step, 0)

    def split_loop(body):
        def step(d, carry):
            body(lax.rem(s + 1 + d, splits))
            return carry
        lax.fori_loop(0, splits - 1, step, 0)

    barrier = pltpu.get_barrier_semaphore()

    def greet(cc, sp):
        pl.semaphore_signal(barrier, inc=1, device_id=(cc, sp), device_id_type=MESH)

    chan_loop(lambda q: greet(q, s))
    split_loop(lambda p: greet(c, p))
    pl.semaphore_wait(barrier, chans + splits - 2)

    copy_o = remote(omega, part_o, p_send.at[0], p_recv.at[0], c, partner)
    copy_h = remote(hamil, part_h, p_send.at[1], p_recv.at[1], c, partner)
    copy_o.start()
    copy_h.start()

    own_cols = pl.ds(pl.multiple_of(s * height, height), height)
    down = lax.broadcasted_iota(jnp.int32, (height, height), 0)
    over = lax.broadcasted_iota(jnp.int32, (height, height), 1)
    mask = jnp.where(phs[...] != 0.0, 1.0, 0.0)
    lower = jnp.where(down <= over, 1.0, 0.0).astype(BF16)
    count = dot(jnp.broadcast_to(mask, (16, height)).astype(BF16), lower)[0:1]
    rank = jnp.where(mask > 0.0, count - 1.0, -1.0)
    lane_of = jnp.where(mask > 0.0, count - 1.0 + (s * active).astype(F32), -1.0)
    pick = lax.broadcasted_iota(jnp.int32, (wide, height), 0).astype(F32)
    pick = jnp.where(pick == lane_of, 1.0, 0.0)
    meta[...] = jnp.zeros_like(meta)
    meta[0:1, :] = permr[:, own_cols].astype(F32)
    meta[1:2, :] = ccr[:, own_cols]
    chosen = lax.dot_general(meta[...], pick, NT, precision=lax.Precision.HIGHEST,
                             preferred_element_type=F32)
    meta[0:2, :wide] = chosen[0:2]
    meta[2:3, :] = pp[...]

    def m1(p, frm):
        return remote(meta, meta1.at[frm], m1_send.at[p], m1_recv.at[frm], c, p)
    split_loop(lambda p: m1(p, s).start())
    meta1[s] = meta[...]

    turned = jnp.where(down == sor[...], 1.0, 0.0)
    order_t[...] = turned.astype(BF16)
    order[...] = turned.T.astype(BF16)
    colvec[:, 0:1] = jnp.sum(jnp.where(down == over, pp[...], 0.0), axis=1, keepdims=True)
    colvec[:, 1:2] = jnp.sum(jnp.where(down == over, rcr[...], 0.0), axis=1, keepdims=True)

    tile = 256
    def sort_tile(n, carry):
        cols = pl.ds(pl.multiple_of(n * tile, tile), tile)
        got = dot(order[...], omega[:, cols]).astype(BF16)
        sorted_r[:, :slots, cols] = got.reshape(chans, slots, tile)
        got = dot(order[...], hamil[:, cols]).astype(BF16)
        sorted_r[:, slots:, cols] = got.reshape(chans, slots, tile)
        return carry
    lax.fori_loop(0, breadth // tile, sort_tile, 0)

    split_loop(lambda p: m1(p, p).wait_recv())
    sums = meta1[0] + meta1[1] + meta1[2] + meta1[3]
    cols_row, act_cc = sums[0:1, :wide], sums[1:2, :wide]
    for q in range(chans):
        meta2s[q] = jnp.zeros(meta2s.shape[1:], F32)
        meta2s[q, 1:2, :slots] = rank[:, q * slots : (q + 1) * slots]
        meta2s[q, 0:1, :] = cols_row

    def m2(q, frm):
        return remote(meta2s.at[q], meta2.at[frm], m2_send.at[q], m2_recv.at[frm], q, s)
    chan_loop(lambda q: m2(q, c).start())
    meta2[c] = meta2s[c]

    rungs = chans // 2
    z, y = c // 2, lax.rem(c, 2)

    def copy_y(to):
        return remote(send_y.at[to], recv_y.at[to], y_send.at[to], y_recv.at[to],
                      z * 2 + 1 - y, s)

    def copy_a(to, frm):
        return remote(send_a.at[to], recv_a.at[frm], a_send.at[to], a_recv.at[frm],
                      to * 2 + y, s)

    def copy_l(q, frm):
        return remote(send_l.at[q], recv_l.at[frm], l_send.at[q], l_recv.at[frm], q, s)

    def pack_rows(q):
        take = lax.broadcasted_iota(jnp.int32, (active, slots), 0).astype(F32)
        take = jnp.where(take == meta2[q, 1:2, :slots], 1.0, 0.0).astype(BF16)
        return dot(take, sorted_r[q, :slots]), dot(take, sorted_r[q, slots:])

    def pack_left(q, to):
        gate = lax.broadcasted_iota(jnp.int32, (breadth, wide), 0).astype(F32)
        gate = jnp.where(gate == meta2[q, 0:1, :wide], 1.0, 0.0).astype(BF16)
        to[q] = dot(sorted_r[q], gate).astype(BF16)

    def to_side(d, carry):
        to = lax.rem(z + 1 + d, rungs)
        q = to * 2 + 1 - y
        m2(q, q).wait_recv()
        got_o, got_h = pack_rows(q)
        send_y[to, :active] = got_o.astype(BF16)
        send_y[to, active:] = got_h.astype(BF16)
        copy_y(to).start()
        return carry
    lax.fori_loop(0, rungs, to_side, 0)

    def along(to, out):
        got_o, got_h = pack_rows(to * 2 + y)
        copy_y(to).wait_recv()
        out[to, :active] = (got_o + recv_y[to, :active].astype(F32)).astype(BF16)
        out[to, active:] = (got_h + recv_y[to, active:].astype(F32)).astype(BF16)

    def along_send(d, carry):
        to = lax.rem(z + 1 + d, rungs)
        m2(to * 2 + y, to * 2 + y).wait_recv()
        along(to, send_a)
        copy_a(to, z).start()
        return carry
    lax.fori_loop(0, rungs - 1, along_send, 0)

    def left_send(q):
        pack_left(q, send_l)
        copy_l(q, c).start()
    chan_loop(left_send)
    pack_left(c, recv_l)
    along(z, recv_a)

    span = height
    for k in range(splits):
        cols = slice(k * span, (k + 1) * span)
        sgn = meta1[k, 2:3, :]
        scal_o[:, cols] = (omega[:, cols].astype(F32) * sgn).astype(BF16)
        scal_h[:, cols] = (hamil[:, cols].astype(F32) * sgn).astype(BF16)

    cc_parts[...] = jnp.zeros_like(cc_parts)
    first = ccr[...].astype(BF16).astype(F32)
    second = (ccr[...] - first).astype(BF16).astype(F32)
    third = ccr[...] - first - second
    cc_parts[0:1, :] = first
    cc_parts[1:2, :] = second
    cc_parts[2:3, :] = third

    def invert(n, carry):
        hit = lax.broadcasted_iota(jnp.int32, (tile, breadth), 0) + n * tile
        hit = jnp.where(hit == permr[...], 1.0, 0.0).astype(BF16)
        val = lax.dot_general(cc_parts[...].astype(BF16), hit, NT, preferred_element_type=F32)
        cc_inv[:, pl.ds(pl.multiple_of(n * tile, tile), tile)] = jnp.sum(
            val, axis=0, keepdims=True)
        return carry
    lax.fori_loop(0, breadth // tile, invert, 0)
    slot_of = lax.broadcasted_iota(jnp.int32, (active, height), 0).astype(F32)
    act_rc = jnp.sum(jnp.where(slot_of == rank, rcr[...], 0.0), axis=1, keepdims=True)
    signs = jnp.sum(jnp.where(slot_of == rank, phs[...], 0.0), axis=1, keepdims=True)

    acc[...] = recv_a[z].astype(F32)

    def add_rows(d, carry):
        frm = lax.rem(z + 1 + d, rungs)
        copy_a(frm, frm).wait_recv()
        acc[...] += recv_a[frm].astype(F32)
        return carry
    lax.fori_loop(0, rungs - 1, add_rows, 0)
    coef_a = act_rc * cc_inv[...]
    right_s[1] = (-signs * (coef_a * acc[:active]).astype(BF16).astype(F32)).astype(BF16)
    right_s[0] = (signs * (coef_a * acc[active:]).astype(BF16).astype(F32)).astype(BF16)

    def place(p):
        return rights.at[:, pl.ds(pl.multiple_of(p * active, active), active), :]

    away = lax.rem(s + 2, splits)
    partner_away = lax.rem(partner + 2, splits)

    def copy_r(src, block, p, which):
        return remote(src, place(block), r_send.at[which], r_recv.at[block], c, p)
    copy_r(right_s, s, away, 0).start()
    copy_r(right_s, s, partner, 1).start()
    rights[:, pl.ds(pl.multiple_of(s * active, active), active), :] = right_s[...]

    def make_bars(q):
        rows = pl.ds(pl.multiple_of(q * slots, slots), slots)
        coef = colvec[rows, 1:2] * act_cc
        bars[rows, :wide] = (coef * recv_l[q, :slots].astype(F32)).astype(BF16)
        bars[rows, wide:] = (coef * recv_l[q, slots:].astype(F32)).astype(BF16)

    def bars_from(q):
        copy_l(q, q).wait_recv()
        make_bars(q)
    chan_loop(bars_from)
    make_bars(c)
    copy_r(right_s, away, away, 0).wait_recv()
    copy_r(place(away), away, partner, 2).start()
    copy_r(right_s, partner, partner, 1).wait_recv()
    copy_r(right_s, partner_away, partner, 2).wait_recv()

    def copy_b(q, frm):
        return remote(back_s.at[q], back_r.at[frm], b_send.at[q], b_recv.at[frm], q, s)

    def product(q, to):
        rows = pl.ds(pl.multiple_of(q * slots, slots), slots)
        val = dot(bars[rows, :wide], rights[0]) + dot(bars[rows, wide:], rights[1])
        to[q] = (colvec[rows, 1:2] * cc_inv[...] * val).astype(BF16)

    def product_send(q):
        product(q, back_s)
        copy_b(q, c).start()
    chan_loop(product_send)
    product(c, back_r)

    copy_o.wait_recv()
    copy_h.wait_recv()
    own = pl.ds(pl.multiple_of(s * span, span), span)
    oth = pl.ds(pl.multiple_of(partner * span, span), span)

    def cross(m, carry):
        def half_tile(t, carry):
            cols = pl.ds(pl.multiple_of((far + m) * span + t * tile, tile), tile)
            val = dot(scal_o[:, own], hamil[:, cols]) - dot(scal_h[:, own], omega[:, cols])
            val = val + dot(scal_o[:, oth], part_h[:, cols]) - dot(scal_h[:, oth], part_o[:, cols])
            ladder[:, cols] = val
            x_send[m, :, pl.ds(pl.multiple_of(t * tile, tile), tile)] = val.astype(BF16)
            return carry
        return lax.fori_loop(0, span // tile, half_tile, carry)

    def copy_x(m, frm):
        return remote(x_send.at[m], x_recv.at[frm], x_ss.at[m], x_rs.at[frm], c, far + m)
    core = lax.rem(s, 2)
    for m in range(2):
        cross(m, 0)
        copy_x(m, core).start()

    def same(t, carry):
        rows = pl.ds(pl.multiple_of(t * tile, tile), tile)
        val = lax.dot_general(scal_o[...], part_h[rows], NT, preferred_element_type=F32)
        val = val + lax.dot_general(scal_h[...], part_o[rows], NT, preferred_element_type=F32)
        ladder[:, pl.ds(pl.multiple_of(partner * span + t * tile, tile), tile)] = val
        val = lax.dot_general(scal_o[...], hamil[rows], NT, preferred_element_type=F32)
        val = val + lax.dot_general(scal_h[...], omega[rows], NT, preferred_element_type=F32)
        ladder[:, pl.ds(pl.multiple_of(s * span + t * tile, tile), tile)] = val
        return carry
    lax.fori_loop(0, span // tile, same, 0)

    for m in range(2):
        copy_x(m, m).wait_recv()
        def flip(t, carry):
            val = x_recv[m, :, pl.ds(pl.multiple_of(t * tile, tile), tile)]
            cols = pl.ds(pl.multiple_of((far + m) * span, span), span)
            ladder[pl.ds(pl.multiple_of(t * tile, tile), tile), cols] += val.astype(F32).T
            return carry
        lax.fori_loop(0, span // tile, flip, 0)

    chan_loop(lambda q: copy_b(q, q).wait_recv())

    degeneracy = (2 * (c // 2) + 1).astype(F32)
    weight = degeneracy * colvec[:, 0:1]

    def finish(n, carry):
        cols = pl.ds(pl.multiple_of(n * tile, tile), tile)
        total = ladder[:, cols] + dot(order_t[...], back_r[:, :, cols].reshape(height, tile))
        z_out[:, cols] = total.astype(BF16)
        ob1[s, pl.ds(n, 1), :] = jnp.sum(weight * total, axis=0, keepdims=True)
        return carry
    lax.fori_loop(0, breadth // tile, finish, 0)

    def copy_o1(p, frm):
        return remote(ob1.at[s], ob1.at[frm], o1_send.at[p], o1_recv.at[frm], c, p)
    split_loop(lambda p: copy_o1(p, s).start())
    split_loop(lambda p: copy_o1(p, p).wait_recv())
    ob2[c] = ob1[0] + ob1[1] + ob1[2] + ob1[3]

    def copy_o2(q, frm):
        return remote(ob2.at[c], ob2.at[frm], o2_send.at[q], o2_recv.at[frm], q, s)
    chan_loop(lambda q: copy_o2(q, c).start())
    chan_loop(lambda q: copy_o2(q, q).wait_recv())
    whole = ob2[0]
    for q in range(1, chans):
        whole = whole + ob2[q]
    ob_out[...] = whole * norm

    split_loop(lambda p: m1(p, s).wait_send())
    copy_r(right_s, s, away, 0).wait_send()
    copy_r(right_s, s, partner, 1).wait_send()
    copy_r(place(away), away, partner, 2).wait_send()
    split_loop(lambda p: copy_o1(p, s).wait_send())
    copy_o.wait_send()
    copy_h.wait_send()
    for m in range(2):
        copy_x(m, core).wait_send()

    def sent(q):
        m2(q, c).wait_send()
        copy_l(q, c).wait_send()
        copy_b(q, c).wait_send()
        copy_o2(q, c).wait_send()
    chan_loop(sent)

    def sent_rows(d, carry):
        copy_a(lax.rem(z + 1 + d, rungs), z).wait_send()
        return carry
    lax.fori_loop(0, rungs - 1, sent_rows, 0)

    def sent_side(d, carry):
        copy_y(d).wait_send()
        return carry
    lax.fori_loop(0, rungs, sent_side, 0)


def on_device_fused(omega, hamil, pp_sign, ph_sign, row_coef, col_coef, col_perm, send_order):
    chans, splits = lax.axis_size("chan"), lax.axis_size("split")
    _, height, breadth = omega.shape
    slots, active = height // chans, height // 16
    wide = active * splits
    rungs = chans // 2
    weight_sq = sum((2 * (i // 2) + 1) ** 2 for i in range(chans))
    norm = 1.0 / math.sqrt(breadth * weight_sq)
    vm = pl.BlockSpec(memory_space=pltpu.VMEM)
    dma = pltpu.SemaphoreType.DMA
    z_out, one_body = pl.pallas_call(
        functools.partial(fused, norm),
        out_shape=(jax.ShapeDtypeStruct((height, breadth), BF16),
                   jax.ShapeDtypeStruct((8, breadth // 8), F32)),
        in_specs=[vm] * 8,
        out_specs=(vm, vm),
        scratch_shapes=[
            pltpu.VMEM((height, breadth), BF16), pltpu.VMEM((height, breadth), BF16),
            pltpu.VMEM((height, breadth), BF16), pltpu.VMEM((height, breadth), BF16),
            pltpu.VMEM((splits, 8, height), F32),
            pltpu.VMEM((chans, 8, wide), F32), pltpu.VMEM((chans, 8, wide), F32),
            pltpu.VMEM((chans, 2 * slots, breadth), BF16),
            pltpu.VMEM((rungs, 2 * active, breadth), BF16),
            pltpu.VMEM((rungs, 2 * active, breadth), BF16),
            pltpu.VMEM((chans, 2 * slots, wide), BF16),
            pltpu.VMEM((chans, 2 * slots, wide), BF16),
            pltpu.VMEM((height, breadth), F32),
            pltpu.VMEM((2, height, height), BF16), pltpu.VMEM((2, height, height), BF16),
            pltpu.VMEM((2 * active, breadth), F32),
            pltpu.VMEM((2, wide, breadth), BF16),
            pltpu.VMEM((height, 2 * wide), BF16),
            pltpu.VMEM((chans, slots, breadth), BF16),
            pltpu.VMEM((chans, slots, breadth), BF16),
            pltpu.VMEM((splits, 8, breadth // 8), F32),
            pltpu.VMEM((chans, 8, breadth // 8), F32),
            pltpu.VMEM((2, active, breadth), BF16),
            pltpu.VMEM((rungs, 2 * active, breadth), BF16),
            pltpu.VMEM((rungs, 2 * active, breadth), BF16),
            pltpu.VMEM((8, height), F32),
            pltpu.VMEM((16, breadth), F32),
            pltpu.VMEM((1, breadth), F32),
            pltpu.VMEM((height, 128), F32),
            pltpu.VMEM((height, height), BF16), pltpu.VMEM((height, height), BF16),
            dma((2,)), dma((2,)), dma((splits,)), dma((splits,)),
            dma((chans,)), dma((chans,)), dma((chans,)), dma((chans,)),
            dma((chans,)), dma((chans,)), dma((2,)), dma((2,)),
            dma((splits,)), dma((splits,)), dma((chans,)), dma((chans,)),
            dma((splits,)), dma((splits,)), dma((chans,)), dma((chans,)),
            dma((rungs,)), dma((rungs,)),
        ],
        compiler_params=pltpu.CompilerParams(
            collective_id=0, has_side_effects=True, vmem_limit_bytes=58 * 2**20),
    )(omega[0], hamil[0], pp_sign, ph_sign, row_coef, col_coef, col_perm, send_order)
    return z_out[None], one_body.reshape(-1)


def solution(mesh):
    small = mesh.shape["chan"] == 8 and mesh.shape["split"] == 4
    in_specs = (
        P("chan", "split", None),
        P("chan", "split", None),
        P("chan", "split"),
        P("chan", "split"),
        P("chan", "split"),
        P("chan", None),
        P("chan", None),
        P("chan", "split"),
    )
    out_specs = (P("chan", "split", None), P())
    return jax.shard_map(
        on_device_fused if small else on_device, mesh=mesh, in_specs=in_specs, out_specs=out_specs, check_vma=False
    )
```
